32 devices in a mesh: half: 2 (over y), dp: 8 (over z, x), mp: 2 (over core).
Axes of the slice: x: 2, y: 2, z: 4, core: 2. Of those that a mesh axis runs over, the one named last changes fastest.
Arguments:
- tokens: bfloat16 [2, 9216, 768], P('half', 'dp'), may hold values from -6 to 6
- qkv_weight: bfloat16 [2, 768, 3, 768], P('half', None, None, 'mp'), may hold values from -0.21875 to 0.21875
- out_weight: bfloat16 [2, 768, 768], P('half', 'mp'), may hold values from -0.875 to 0.875
- up_weight: bfloat16 [2, 768, 3072], P('half', None, 'mp'), may hold values from -0.21875 to 0.21875
- down_weight: bfloat16 [2, 3072, 768], P('half', 'mp'), may hold values from -0.109375 to 0.109375
- norm_gains: float32 [2, 2, 768], P('half'), may hold values from 0.1 to 1.9
- cross_gain: float32 [768], replicated, may hold values from 0.1 to 1.9
- cross_query_matrix: bfloat16 [768, 768], P(None, 'mp'), may hold values from -0.21875 to 0.21875
- cross_keyval: bfloat16 [768, 2, 768], P(None, None, 'mp'), may hold values from -0.21875 to 0.21875
- cross_out: bfloat16 [768, 768], P('mp'), may hold values from -0.875 to 0.875
- slot_image: int32 [144], replicated, may hold values from 0 to 15, as said below
- slot_length: int32 [144], replicated, may hold values from 0 to 64, as said below
- cotangent: bfloat16 [2, 9216, 768], P('half', 'dp'), may hold values from -6 to 6
Outputs:
- layer_out: bfloat16 [2, 9216, 768], P('half', 'dp')
- grad_tokens: float32 [2, 9216, 768], P('half', 'dp')
- grad_qkv: float32 [2, 768, 3, 768], P('half', 'dp', None, 'mp')
- grad_out: float32 [2, 768, 768], P('half', 'mp', 'dp')
- grad_up: float32 [2, 768, 3072], P('half', 'dp', 'mp')
- grad_down: float32 [2, 3072, 768], P('half', 'mp', 'dp')
- grad_gains: float32 [2, 2, 768], P('half', None, 'dp')
- grad_cross_gain: float32 [768], P('dp')
- grad_cross_query: float32 [768, 768], P('dp', 'mp')
- grad_cross_keyval: float32 [768, 2, 768], P('dp', None, 'mp')
- grad_cross_out: float32 [768, 768], P('mp', 'dp')
The draws below stay inside these ranges and needn't reach their ends.
Inputs may be any that keep to these rules, and one draw needn't show every extreme that they name: `slot_image`: entry k * 18 + s names the image of the caption in slot s of dp index k of the caption tower, 0 in empty slots. Images i * 2 to i * 2 + 1 are those of dp index i of the image tower. Every image is named by exactly 8 filled slots; every caption dp index k has exactly 16 filled slots, all naming images of image dp indices (k - o) modulo the number of dp indices for o from 0 to 3, at most 6 of them for each o, and that most is reached in every draw. `slot_length`: 0 exactly in empty slots, 1 or more in filled ones; every caption dp index has a caption of 64 tokens.
All inputs are finite; a program needn't handle non-finite values.
Results may differ from the reference program's by a relative error of at most 0.015.
The reference program's roundings to bfloat16 on the way count: a program that leaves them out, or rounds other values in their place, can miss the bound.
Values may be sent and summed in bfloat16 or wider, within the bound.
A program may use at most 256 MiB of HBM per device.

```python
import jax
import jax.numpy as jnp
from jax import lax

D = 768
HEADS = 12
HEAD = 64
FF = 3072
PATCH = 576
SLOT = 64
CAPS = 8
SPREAD = 4
IMG_DEV = 2
TOTAL = 9216
N_DP = 8


def caption_plan(key):
    per_owner = CAPS * IMG_DEV
    slot_count = IMG_DEV * PATCH // SLOT
    pattern = jnp.array([3, 2, 1, 2], jnp.int32)
    rotate = jax.random.randint(jax.random.fold_in(key, 11), (), 0, 4)
    owners = jnp.arange(N_DP)
    offsets = jnp.arange(SPREAD)
    counts = IMG_DEV * pattern[(owners[:, None] + 3 * offsets[None, :] + rotate) % 4]
    starts = jnp.cumsum(counts, axis=1) - counts

    def owner_order(subkey):
        return jax.random.permutation(subkey, per_owner)

    def seat_order(subkey):
        return jax.random.permutation(subkey, slot_count)
    orders = jax.vmap(owner_order)(jax.random.split(jax.random.fold_in(key, 12), N_DP))
    sources = (owners[:, None] - offsets[None, :]) % N_DP
    taken_count = counts[sources, offsets[None, :]]
    begin_at = starts[sources, offsets[None, :]]
    places = jnp.arange(3 * IMG_DEV)
    live_mask = places[None, None, :] < taken_count[:, :, None]
    pick_index = jnp.minimum(begin_at[:, :, None] + places[None, None, :], per_owner - 1)
    local_ids = jnp.take_along_axis(orders[sources], pick_index, axis=2)
    image_ids = sources[:, :, None] * IMG_DEV + local_ids // CAPS
    live_mask = live_mask.reshape(N_DP, -1)
    image_ids = image_ids.reshape(N_DP, -1)
    ranking = jnp.argsort(1 - live_mask.astype(jnp.int32), axis=1, stable=True)
    image_ids = jnp.take_along_axis(image_ids, ranking, axis=1)[:, :per_owner]
    seat_ids = jax.vmap(seat_order)(jax.random.split(jax.random.fold_in(key, 13), N_DP))[:, :per_owner]
    row_ids = jnp.broadcast_to(owners[:, None], seat_ids.shape)
    slot_ids = jnp.zeros((N_DP, slot_count), jnp.int32).at[row_ids, seat_ids].set(image_ids.astype(jnp.int32))
    filled = jnp.zeros((N_DP, slot_count), jnp.int32).at[row_ids, seat_ids].set(1)
    return (slot_ids.reshape(-1), filled, seat_ids[:, 0])


def draw_slot_image(key, part):
    slot_ids, filled, first_seat = caption_plan(jax.random.fold_in(key, 5))
    return slot_ids.astype(jnp.int32)


def draw_slot_length(key, part):
    slot_ids, filled, first_seat = caption_plan(jax.random.fold_in(key, 5))
    slot_count = IMG_DEV * PATCH // SLOT
    divisor = jax.random.randint(jax.random.fold_in(key, 21), (N_DP, slot_count), 1, SLOT + 1)
    length = SLOT // divisor
    length = length.at[jnp.arange(N_DP), first_seat].set(SLOT)
    return (length * filled).reshape(-1).astype(jnp.int32)


def level_of(rng, shape, cuts, low, top_value):
    level, own = 1.0, jax.random.fold_in(rng, 6)
    for axis_at, blocks in cuts:
        heights = jnp.exp(jax.random.uniform(jax.random.fold_in(own, axis_at), (blocks,), jnp.float32, low / len(cuts), top_value / len(cuts)))
        level = level * jnp.repeat(heights, shape[axis_at] // blocks).reshape([-1 if axis == axis_at else 1 for axis in range(len(shape))])
    return level


def scatter_about(rng, shape, spread, reach, pieces=(), kind=jnp.bfloat16):
    values = spread * jax.random.normal(rng, shape, jnp.float32)
    if pieces:
        values = values * level_of(rng, shape, pieces, -0.22, 0.18)
    return jnp.clip(values, -reach, reach).astype(kind)


def setup_inputs(seed: int = 0) -> dict:
    key_list = jax.random.split(jax.random.key(seed), 14)
    return {
        "tokens": scatter_about(key_list[0], (2, TOTAL, D), 1.0, 6.0, ((0, 2), (1, 8))),
        "qkv_weight": scatter_about(key_list[1], (2, D, 3, D), D ** -0.5, 0.21875, ((0, 2), (3, 2))),
        "out_weight": scatter_about(key_list[2], (2, D, D), (D // 16) ** -0.5, 0.875, ((0, 2), (1, 2))),
        "up_weight": scatter_about(key_list[3], (2, D, FF), D ** -0.5, 0.21875, ((0, 2), (2, 2))),
        "down_weight": scatter_about(key_list[4], (2, FF, D), FF ** -0.5, 0.109375, ((0, 2), (1, 2))),
        "norm_gains": jnp.clip(1.0 + 0.18 * jax.random.normal(key_list[5], (2, 2, D), jnp.float32), 0.1, 1.9),
        "cross_gain": jnp.clip(1.0 + 0.18 * jax.random.normal(key_list[6], (D,), jnp.float32), 0.1, 1.9),
        "cross_query_matrix": scatter_about(key_list[7], (D, D), D ** -0.5, 0.21875, ((1, 2),)),
        "cross_keyval": scatter_about(key_list[8], (D, 2, D), D ** -0.5, 0.21875, ((2, 2),)),
        "cross_out": scatter_about(key_list[9], (D, D), (D // 16) ** -0.5, 0.875, ((0, 2),)),
        "slot_image": draw_slot_image(jax.random.fold_in(key_list[13], 71), 0),
        "slot_length": draw_slot_length(jax.random.fold_in(key_list[13], 71), 0),
        "cotangent": scatter_about(key_list[12], (2, TOTAL, D), 1.0, 6.0, ((0, 2), (1, 8))),
    }


@jax.custom_vjp
def low(v):
    return lax.optimization_barrier(v.astype(jnp.bfloat16)).astype(jnp.float32)

@jax.custom_vjp
def low_back(v):
    return v

def low_keep(v):
    return (low(v), None)

def low_pass(kept, grad):
    return (grad,)

def back_keep(v):
    return (v, None)

def back_low(kept, grad):
    return (low(grad),)
low.defvjp(low_keep, low_pass)
low_back.defvjp(back_keep, back_low)
EPS = 1e-06
NEG = -1e+30
HIGH = lax.Precision.HIGHEST

def matmul(left, right):
    return jnp.dot(left, right, precision=HIGH, preferred_element_type=jnp.float32)

def norm_rows(inputs, gain):
    mean = lax.optimization_barrier(jnp.mean(inputs, axis=-1, keepdims=True))
    centred = inputs - mean
    return centred * lax.rsqrt(lax.optimization_barrier(jnp.mean(centred * centred, axis=-1, keepdims=True)) + EPS) * gain

def attend(queries, key_rows, value_rows, keep_mask):
    factor = queries.shape[-1] ** (-0.5)
    scores = low_back(jnp.einsum('blhe,bmhe->bhlm', queries, key_rows, precision=HIGH) * factor)
    scores = jnp.where(keep_mask[:, None], scores, NEG)
    probability = jax.nn.softmax(scores, axis=-1)
    return low(low_back(jnp.einsum('bhlm,bmhe->blhe', low(probability), value_rows, precision=HIGH)))

def feed_forward(hidden, gain, up_proj, down_proj):
    normed = low(norm_rows(hidden, gain))
    upward = low_back(matmul(normed, up_proj))
    active = low(jax.nn.gelu(upward, approximate=False))
    return hidden + low_back(matmul(active, down_proj))

def forward(tokens, qkv_weight, out_weight, up_weight, down_weight, norm_gains, cross_gain, cross_query_matrix, cross_keyval, cross_out, slot_image, slot_length):
    images = N_DP * IMG_DEV
    cap_dev = IMG_DEV * PATCH // SLOT
    model_width = HEADS * HEAD
    image_rows = tokens[0]
    caption_rows = tokens[1]
    position = jnp.arange(SLOT)
    normed = low(norm_rows(image_rows, norm_gains[0, 0]))
    qkv_rows = low(low_back(matmul(normed, qkv_weight[0].reshape(model_width, 3 * model_width))))
    qkv_rows = qkv_rows.reshape(images, 1, PATCH, 3, HEADS, HEAD)
    open_mask = jnp.ones((1, PATCH, PATCH), bool)

    def image_block(block_qkv):
        return attend(block_qkv[:, :, 0], block_qkv[:, :, 1], block_qkv[:, :, 2], open_mask)
    attended = lax.map(jax.checkpoint(image_block), qkv_rows).reshape(images * PATCH, model_width)
    hidden = image_rows + low_back(matmul(attended, out_weight[0]))
    image_out = feed_forward(hidden, norm_gains[0, 1], up_weight[0], down_weight[0])
    normed = low(norm_rows(caption_rows, norm_gains[1, 0]))
    qkv_rows = low(low_back(matmul(normed, qkv_weight[1].reshape(model_width, 3 * model_width))))
    qkv_rows = qkv_rows.reshape(N_DP, cap_dev, SLOT, 3, HEADS, HEAD)
    lengths = slot_length.reshape(N_DP, cap_dev)
    causal = (position[None, :] <= position[:, None])[None]

    def caption_block(member):
        block_qkv, block_lengths = member
        inside = (position[None, None, :] < block_lengths[:, None, None]) | (position[None, None, :] == 0)
        return attend(block_qkv[:, :, 0], block_qkv[:, :, 1], block_qkv[:, :, 2], causal & inside)
    attended = lax.map(jax.checkpoint(caption_block), (qkv_rows, lengths)).reshape(N_DP * cap_dev * SLOT, model_width)
    hidden = caption_rows + low_back(matmul(attended, out_weight[1]))
    cross_in = low(norm_rows(hidden, cross_gain))
    cross_attention_rows = low(low_back(matmul(cross_in, cross_query_matrix))).reshape(N_DP, cap_dev, SLOT, HEADS, HEAD)
    image_kv = low(low_back(matmul(image_rows, cross_keyval.reshape(model_width, 2 * model_width))))
    image_kv = image_kv.reshape(images, PATCH, 2, HEADS, HEAD)
    slot_images = slot_image.reshape(N_DP, cap_dev)
    filled = (lengths > 0).astype(jnp.float32)
    full_mask = jnp.ones((1, SLOT, PATCH), bool)

    def cross_block(member):
        block_query, block_images, block_filled = member
        chosen = jnp.take(image_kv, block_images.astype(jnp.int32), axis=0)
        output = attend(block_query, chosen[:, :, 0], chosen[:, :, 1], full_mask)
        return output * block_filled[:, None, None, None]
    attention_context = lax.map(jax.checkpoint(cross_block), (cross_attention_rows, slot_images, filled)).reshape(N_DP * cap_dev * SLOT, model_width)
    hidden = hidden + low_back(matmul(attention_context, cross_out))
    caption_out = feed_forward(hidden, norm_gains[1, 1], up_weight[1], down_weight[1])
    return jnp.stack([image_out, caption_out])

def reference(tokens, qkv_weight, out_weight, up_weight, down_weight, norm_gains, cross_gain, cross_query_matrix, cross_keyval, cross_out, slot_image, slot_length, cotangent):
    floats = tuple((member.astype(jnp.float32) for member in (tokens, qkv_weight, out_weight, up_weight, down_weight, norm_gains, cross_gain, cross_query_matrix, cross_keyval, cross_out)))

    def layer(*params):
        return forward(*params, slot_image, slot_length)
    result, pull = jax.vjp(layer, *floats)
    grads = pull(cotangent.astype(jnp.float32))
    return (result.astype(jnp.bfloat16), grads[0], grads[1], grads[2], grads[3], grads[4], grads[5], grads[6], grads[7], grads[8], grads[9])
```

```python
import functools

import jax
import jax.numpy as jnp
from jax import lax
from jax.experimental import pallas as pl
from jax.experimental.pallas import tpu as pltpu
from jax.sharding import PartitionSpec as P

HEAD = 64
PATCH = 576
SLOT = 64
SPREAD = 4
IMG_DEV = 2
QCAP = 6
CAPS = 8

EPS = 1e-06
NEG = -1e30
SCALE = HEAD**-0.5

F32 = jnp.float32
BF16 = jnp.bfloat16
VMEM = pl.BlockSpec(memory_space=pltpu.VMEM)
SMEM = pl.BlockSpec(memory_space=pltpu.SMEM)
ANY = pl.BlockSpec(memory_space=pl.ANY)
LIMIT = 56 * 1024 * 1024


def dot(a, b):
    return lax.dot_general(a, b, (((1,), (0,)), ((), ())), preferred_element_type=F32)


def dot_nt(a, b):
    return lax.dot_general(a, b, (((1,), (1,)), ((), ())), preferred_element_type=F32)


def dot_tn(a, b):
    return lax.dot_general(a, b, (((0,), (0,)), ((), ())), preferred_element_type=F32)


def norm_stats(v):
    mean = jnp.mean(v, axis=-1, keepdims=True)
    centred = v - mean
    rstd = lax.rsqrt(jnp.mean(centred * centred, axis=-1, keepdims=True) + EPS)
    return centred * rstd, rstd


def norm_rows(v, gain):
    return norm_stats(v)[0] * gain


def norm_back(v, gain, dn):
    x_hat, rstd = norm_stats(v)
    dg = dn * gain
    m1 = jnp.mean(dg, axis=-1, keepdims=True)
    m2 = jnp.mean(dg * x_hat, axis=-1, keepdims=True)
    return (dg - m1 - x_hat * m2) * rstd, jnp.sum(dn * x_hat, axis=0, keepdims=True)


def head_masks():
    lane = lax.broadcasted_iota(jnp.int32, (1, 2 * HEAD), 1)
    first = (lane < HEAD).astype(F32)
    return first.astype(BF16), (1.0 - first).astype(BF16)


def three(ref, half):
    return jnp.concatenate([ref[3 * half], ref[3 * half + 1], ref[3 * half + 2]], axis=1)


def attend(q, k, v, masks, bias):
    v_t = v.T
    outs, sums = [], []
    for h in range(2):
        s = dot_nt(k, q * masks[h])
        if bias is not None:
            s = s + bias
        top = jnp.max(s, axis=0, keepdims=True)
        e = jnp.exp(s - top)
        total = jnp.sum(e, axis=0, keepdims=True)
        p = (e * (1.0 / total)).astype(BF16)
        outs.append(dot(v_t[h * HEAD : (h + 1) * HEAD], p))
        sums.append(top + jnp.log(total))
    return jnp.concatenate(outs, axis=0).T.astype(BF16), sums


def attend_back(q, k, v, do, masks, bias, sums):
    k_t = k.T
    dqs = []
    dk = dv = None
    for h in range(2):
        qh = q * masks[h]
        doh = do * masks[h]
        s = dot_nt(k, qh)
        if bias is not None:
            s = s + bias
        if sums is None:
            e = jnp.exp(s - jnp.max(s, axis=0, keepdims=True))
            p = e * (1.0 / jnp.sum(e, axis=0, keepdims=True))
        else:
            p = jnp.exp(s - sums[h])
        dp = dot_nt(v, doh)
        delta = jnp.sum(p * dp, axis=0, keepdims=True)
        ds = (p * (dp - delta)).astype(BF16)
        dv_h = dot(p.astype(BF16), doh)
        dk_h = dot(ds, qh)
        dv = dv_h if dv is None else dv + dv_h
        dk = dk_h if dk is None else dk + dk_h
        dqs.append(dot(k_t[h * HEAD : (h + 1) * HEAD], ds))
    dq = (jnp.concatenate(dqs, axis=0) * SCALE).T
    return dq.astype(BF16), dk.astype(BF16), dv.astype(BF16)


GROUP = 3 * SLOT


def caption_bias(meta, bias):
    key = lax.broadcasted_iota(jnp.int32, (GROUP, GROUP), 0)
    query = lax.broadcasted_iota(jnp.int32, (GROUP, GROUP), 1)
    key_slot, key_pos = key >> 6, key & 63
    same = (key_slot == (query >> 6)) & (key_pos <= (query & 63))
    for g in range(3):
        limit = jnp.where(
            key_slot == 0,
            meta[1 + 3 * g],
            jnp.where(key_slot == 1, meta[2 + 3 * g], meta[3 + 3 * g]),
        )
        keep = same & ((key_pos < limit) | (key_pos == 0))
        bias[g] = jnp.where(keep, 0.0, NEG)


def pre_kernel(meta, x, gain, gain_cross, w_own, w_oth, o_own, o_oth, a_ref, r_ref, n_ref, q_ref, k_ref, v_ref, t_ref, bias):
    source = x[...].astype(F32)
    normed = norm_rows(source, gain[0:1, :]).astype(BF16)
    n_ref[...] = normed

    @pl.when(meta[0] == 0)
    def _():
        a_ref[...] = normed
        r_ref[...] = source

    @pl.when(meta[0] == 1)
    def _():
        caption_bias(meta, bias)
        for half, w in ((0, w_own), (1, w_oth)):
            for j, ref in enumerate((q_ref, k_ref, v_ref)):
                rows = dot(n_ref[...], w[j]).astype(BF16)
                if j == 0:
                    rows = rows * SCALE
                for p in range(3):
                    ref[3 * half + p] = rows[:, p * 128 : (p + 1) * 128]
        masks = head_masks()

        @pl.loop(0, 6)
        def _(p):
            for g in range(3):
                at = slice(g * GROUP, (g + 1) * GROUP)
                out, unused = attend(q_ref[p, at], k_ref[p, at], v_ref[p, at], masks, bias[g])
                t_ref[p, at] = out

        hidden = x[...].astype(F32) + dot(three(t_ref, 0), o_own[...]) + dot(three(t_ref, 1), o_oth[...])
        r_ref[...] = hidden
        a_ref[...] = norm_rows(hidden, gain_cross[...]).astype(BF16)


def mid_kernel(meta, a_ref, b_ref, r_ref, gain, w_own, w_oth, o_own, o_oth, q_ref, k_ref, v_ref, c_ref, s_ref, m_ref, f_ref):
    rows_in = a_ref.shape[0]
    for half, w in ((0, w_own), (1, w_oth)):
        for j, (ref, src) in enumerate(((q_ref, a_ref), (k_ref, b_ref), (v_ref, b_ref))):
            rows = dot(src[...], w[j]).astype(BF16)
            if j == 0:
                rows = rows * SCALE
            for p in range(3):
                ref[3 * half + p] = rows[:, p * 128 : (p + 1) * 128]
    masks = head_masks()

    @pl.loop(0, 6)
    def _(p):
        out, sums = attend(q_ref[p], k_ref[p], v_ref[p], masks, None)
        c_ref[p] = out
        s_ref[2 * p] = sums[0]
        s_ref[2 * p + 1] = sums[1]

    @pl.when(meta[0] == 1)
    def _():
        for p in range(6):
            c_ref[p, CAPS * SLOT : rows_in] = jnp.zeros((rows_in - CAPS * SLOT, 128), BF16)

    mixed = r_ref[...] + dot(three(c_ref, 0), o_own[...]) + dot(three(c_ref, 1), o_oth[...])
    m_ref[...] = mixed
    f_ref[...] = norm_rows(mixed, gain[1:2, :]).astype(BF16)


def ffn_kernel(last, f_ref, cot, up, down, *rest):
    if last:
        out_in, grad_in, mixed, gain, g_ref, y_ref, gm_ref, gg_ref, acc_out, acc_grad = rest
    else:
        g_ref, acc_out, acc_grad = rest
    step = pl.program_id(0)

    @pl.when(step == 0)
    def _():
        if last:
            acc_out[...] = out_in[...]
            acc_grad[...] = grad_in[...]
        else:
            acc_out[...] = jnp.zeros_like(acc_out)
            acc_grad[...] = jnp.zeros_like(acc_grad)

    upward = dot(f_ref[...], up[...])
    phi = 0.5 * (1.0 + lax.erf(upward * (0.5**0.5)))
    active = (upward * phi).astype(BF16)
    slope = phi + upward * (jnp.exp(-0.5 * upward * upward) * 0.3989422804014327)
    grad_active = dot_nt(cot[...], down[...])
    grad_upward = (grad_active * slope).astype(BF16)
    acc_out[...] += dot(active, down[...])
    g_ref[1] = dot_tn(cot[...], active).astype(BF16)
    g_ref[0] = dot_tn(f_ref[...], grad_upward).astype(BF16)
    acc_grad[...] += dot_nt(grad_upward, up[...])
    if last:

        @pl.when(step == pl.num_programs(0) - 1)
        def _():
            y_ref[...] = (mixed[...] + acc_out[...]).astype(BF16)
            back, gain_grad = norm_back(mixed[...], gain[1:2, :], acc_grad[...])
            gm_ref[...] = cot[...].astype(F32) + back
            gg_ref[...] = gain_grad


def back_kernel(meta, gm_ref, c_ref, s_ref, q_ref, k_ref, v_ref, a_ref, b_ref, w_own, w_oth, o_own, o_oth, g_own, g_oth, da_ref, db_ref, do_ref, dq_ref, dk_ref, dv_ref):
    rows_in = a_ref.shape[0]
    low = gm_ref[...].astype(BF16)
    for half, o, g in ((0, o_own, g_own), (1, o_oth, g_oth)):
        g[0] = dot_tn(low, three(c_ref, half)).astype(BF16)
        rows = dot_nt(low, o[...]).astype(BF16)
        for p in range(3):
            do_ref[3 * half + p] = rows[:, p * 128 : (p + 1) * 128]

    @pl.when(meta[0] == 1)
    def _():
        for p in range(6):
            do_ref[p, CAPS * SLOT : rows_in] = jnp.zeros((rows_in - CAPS * SLOT, 128), BF16)

    masks = head_masks()

    @pl.loop(0, 6)
    def _(p):
        sums = (s_ref[2 * p], s_ref[2 * p + 1])
        dq, dk, dv = attend_back(q_ref[p], k_ref[p], v_ref[p], do_ref[p], masks, None, sums)
        dq_ref[p] = dq
        dk_ref[p] = dk
        dv_ref[p] = dv

    for half, w, g in ((0, w_own, g_own), (1, w_oth, g_oth)):
        dq, dk, dv = three(dq_ref, half), three(dk_ref, half), three(dv_ref, half)
        g[1] = dot_tn(a_ref[...], dq).astype(BF16)
        g[2] = dot_tn(b_ref[...], dk).astype(BF16)
        g[3] = dot_tn(b_ref[...], dv).astype(BF16)
        part_a = dot_nt(dq, w[0])
        part_b = dot_nt(dk, w[1]) + dot_nt(dv, w[2])
        if half == 0:
            da_ref[...] = part_a
            db_ref[...] = part_b
        else:
            da_ref[...] += part_a
            db_ref[...] += part_b


def post_kernel(meta, x, gain, gain_cross, gm_ref, da_ref, db_ref, r_ref, n_ref, q_ref, k_ref, v_ref, t_ref, w_own, w_oth, o_own, o_oth, gt_ref, g_own, g_oth, gg_ref, bias, do_ref, dq_ref, dk_ref, dv_ref, gh_ref):
    @pl.when(meta[0] == 0)
    def _():
        back, gain_grad = norm_back(x[...].astype(F32), gain[0:1, :], da_ref[...] + db_ref[...])
        gt_ref[...] = gm_ref[...] + back
        gg_ref[0:1, :] = gain_grad
        gg_ref[1:2, :] = jnp.zeros_like(gain_grad)

    @pl.when(meta[0] == 1)
    def _():
        caption_bias(meta, bias)
        back, gain_grad = norm_back(r_ref[...], gain_cross[...], da_ref[...])
        gg_ref[1:2, :] = gain_grad
        gh_ref[...] = gm_ref[...] + back
        low = gh_ref[...].astype(BF16)
        for half, o, g in ((0, o_own, g_own), (1, o_oth, g_oth)):
            g[0] = dot_tn(low, three(t_ref, half)).astype(BF16)
            rows = dot_nt(low, o[...]).astype(BF16)
            for p in range(3):
                do_ref[3 * half + p] = rows[:, p * 128 : (p + 1) * 128]
        masks = head_masks()

        @pl.loop(0, 6)
        def _(p):
            for g in range(3):
                at = slice(g * GROUP, (g + 1) * GROUP)
                dq, dk, dv = attend_back(
                    q_ref[p, at], k_ref[p, at], v_ref[p, at], do_ref[p, at], masks, bias[g], None
                )
                dq_ref[p, at] = dq
                dk_ref[p, at] = dk
                dv_ref[p, at] = dv

        total = None
        for half, w, g in ((0, w_own, g_own), (1, w_oth, g_oth)):
            for j, ref in enumerate((dq_ref, dk_ref, dv_ref)):
                rows = three(ref, half)
                g[1 + j] = dot_tn(n_ref[...], rows).astype(BF16)
                part = dot_nt(rows, w[j])
                total = part if total is None else total + part
        back, gain_grad = norm_back(x[...].astype(F32), gain[0:1, :], total)
        gt_ref[...] = gh_ref[...] + back
        gg_ref[0:1, :] = gain_grad


def gather_kernel(table_sizes, out_sizes, idx, *refs):
    tables = refs[: len(table_sizes)]
    outs = refs[len(table_sizes) : len(table_sizes) + len(out_sizes)]
    sems = refs[-1]
    at = 0
    waits = []
    for out, size in zip(outs, out_sizes):
        for row in range(size):
            code = idx[at]
            base = 0
            for table, count in zip(tables, table_sizes):

                @pl.when((code >= base) & (code < base + count))
                def _():
                    pltpu.make_async_copy(table.at[code - base], out.at[row], sems.at[at]).start()

                base += count
            waits.append(pltpu.make_async_copy(tables[0].at[0], out.at[row], sems.at[at]))
            at += 1
    for wait in waits:
        wait.wait()


def gather_slots(idx, tables, out_sizes):
    sizes = tuple(table.shape[0] for table in tables)
    block = tables[0].shape[1:]
    return pl.pallas_call(
        functools.partial(gather_kernel, sizes, tuple(out_sizes)),
        out_shape=[jax.ShapeDtypeStruct((n,) + block, tables[0].dtype) for n in out_sizes],
        in_specs=[SMEM] + [ANY] * len(tables),
        out_specs=[ANY] * len(out_sizes),
        scratch_shapes=[pltpu.SemaphoreType.DMA((sum(out_sizes),))],
        name="gather_slots",
    )(idx, *tables)


def call(kernel, name, outs, scratch, smem_first, *args):
    return pl.pallas_call(
        kernel,
        out_shape=[jax.ShapeDtypeStruct(shape, dtype) for shape, dtype in outs],
        in_specs=([SMEM] if smem_first else []) + [VMEM] * (len(args) - int(smem_first)),
        out_specs=[VMEM] * len(outs),
        scratch_shapes=scratch,
        compiler_params=pltpu.CompilerParams(vmem_limit_bytes=LIMIT),
        name=name,
    )(*args)


def ffn_call(last, ffn_in, cot, up, down, *extra):
    rows, width = ffn_in.shape
    hidden = up.shape[1]
    chunk = hidden // 3
    whole = pl.BlockSpec((rows, width), lambda j: (0, 0))
    in_specs = [
        whole,
        whole,
        pl.BlockSpec((width, chunk), lambda j: (0, j)),
        pl.BlockSpec((chunk, width), lambda j: (j, 0)),
    ]
    g_spec = pl.BlockSpec((2, width, chunk), lambda j: (0, 0, j))
    g_shape = jax.ShapeDtypeStruct((2, width, hidden), BF16)
    wide = jax.ShapeDtypeStruct((rows, width), F32)
    if last:
        in_specs += [whole, whole, whole, pl.BlockSpec(extra[3].shape, lambda j: (0, 0))]
        out_shape = [g_shape, jax.ShapeDtypeStruct((rows, width), BF16), wide, jax.ShapeDtypeStruct((1, width), F32)]
        out_specs = [g_spec, whole, whole, pl.BlockSpec((1, width), lambda j: (0, 0))]
        scratch = [pltpu.VMEM((rows, width), F32)] * 2
    else:
        out_shape = [g_shape, wide, wide]
        out_specs = [g_spec, whole, whole]
        scratch = []
    return pl.pallas_call(
        functools.partial(ffn_kernel, last),
        grid=(3,),
        out_shape=out_shape,
        in_specs=in_specs,
        out_specs=out_specs,
        scratch_shapes=scratch,
        compiler_params=pltpu.CompilerParams(vmem_limit_bytes=LIMIT),
        name="ffn_own" if last else "ffn_other",
    )(ffn_in, cot, up, down, *extra)


def swap_mp(value, captions_only=False):
    if not captions_only:
        return lax.ppermute(value, "mp", [(0, 1), (1, 0)])
    count = lax.axis_size("dp")
    pairs = [((count + d) * 2 + c, (count + d) * 2 + 1 - c) for d in range(count) for c in range(2)]
    return lax.ppermute(value, ("half", "dp", "mp"), pairs)


def caption_shift(value, steps):
    count = lax.axis_size("dp")
    pairs = [
        ((count + d) * 2 + c, (count + (d + steps) % count) * 2 + c) for d in range(count) for c in range(2)
    ]
    return lax.ppermute(value, ("half", "dp", "mp"), pairs)


def reduce_dp(own, arrived):
    count = lax.axis_size("dp")
    me = lax.axis_index("dp")
    lead, rows, cols = own.shape
    bits = count.bit_length() - 1
    shape = (lead,) + (2,) * bits + (rows // count, cols)
    kept, got = own.reshape(shape), arrived.reshape(shape)
    for bit in range(bits):
        axis = bits - bit
        mine = (me >> bit) & 1

        def part(value, which):
            return lax.dynamic_index_in_dim(value, which, axis, keepdims=False).astype(F32)

        send = (part(kept, 1 - mine) + part(got, 1 - mine)).astype(BF16)
        kept = part(kept, mine) + part(got, mine)
        got = lax.ppermute(send, "dp", [(d, d ^ (1 << bit)) for d in range(count)])
        if bit < bits - 1:
            continue
    return kept + got.astype(F32)


def route_tables(slot_image, slot_length, me, c, side, cap_dev):
    total = slot_image.shape[0]
    count = total // cap_dev
    slot = jnp.arange(total)
    home = slot // cap_dev
    filled = slot_length > 0
    image = slot_image
    dest = image // IMG_DEV
    offset = jnp.where(filled, (home - dest) % count, SPREAD)
    core = image % IMG_DEV
    before = slot[None, :] < slot[:, None]
    same_home = home[None, :] == home[:, None]
    same_offset = offset[None, :] == offset[:, None]
    rank = jnp.sum((before & same_home & same_offset).astype(jnp.int32), axis=1)
    place = jnp.sum(
        (before & filled[None, :] & (image[None, :] == image[:, None])).astype(jnp.int32), axis=1
    )
    half_cap = QCAP // 2
    local = slot % cap_dev
    pack_core, pack_row = rank // half_cap, rank % half_cap
    seats = jnp.arange(half_cap)

    def pick(match, code):
        return jnp.sum(jnp.where(match, code[None, :], 0), axis=1)

    offs = jnp.repeat(jnp.arange(1, SPREAD), half_cap)
    rows = jnp.tile(seats, SPREAD - 1)
    mine = (offset[None, :] == offs[:, None]) & (pack_core[None, :] == c) & (pack_row[None, :] == rows[:, None])
    send_idx = pick(mine & (home[None, :] == me), local)
    per_core = cap_dev // 2
    arrived_code = cap_dev + jnp.where(pack_core == c, 0, 9) + (offset - 1) * half_cap + pack_row
    seat = jnp.arange(per_core)
    named = filled & (image == me * IMG_DEV + c)
    hit = jnp.where(
        (seat < CAPS)[:, None],
        named[None, :] & (place[None, :] == seat[:, None]),
        ((~filled) & (home == me) & (rank == c))[None, :],
    )
    work_idx = pick(hit, jnp.where(offset % SPREAD == 0, local, arrived_code))
    work_len = pick(hit, slot_length)
    work_idx = jnp.where(side == 0, c * per_core + seat, work_idx)
    at_core = jnp.where(core == c, 0, per_core) + place
    back_idx = pick(mine & (home[None, :] == (me + offs[:, None]) % count), at_core)
    here = lax.dynamic_slice_in_dim(
        jnp.where(
            filled,
            jnp.where(offset == 0, at_core, cap_dev + jnp.where(pack_core == c, 0, 9) + (offset - 1) * half_cap + pack_row),
            jnp.where(rank == c, 0, per_core) + per_core - 1,
        ),
        me * cap_dev,
        cap_dev,
    )
    spot = jnp.arange(cap_dev)
    home_idx = jnp.where(side == 0, jnp.where(spot // per_core == c, 0, per_core) + spot % per_core, here)
    return send_idx, work_idx, work_len, back_idx, home_idx


def shards(
    tokens,
    qkv_weight,
    out_weight,
    up_weight,
    down_weight,
    norm_gains,
    cross_gain,
    cross_query_matrix,
    cross_keyval,
    cross_out,
    slot_image,
    slot_length,
    cotangent,
):
    count = lax.axis_size("dp")
    side = lax.axis_index("half")
    me = lax.axis_index("dp")
    c = lax.axis_index("mp")
    row_count, width = tokens.shape[1:]
    cap_dev = row_count // SLOT
    per_core = cap_dev // 2
    rows = row_count // 2
    is_image = side == 0

    send_idx, work_idx, work_len, back_idx, home_idx = route_tables(
        slot_image, slot_length, me, c, side, cap_dev
    )
    meta = jnp.concatenate([side[None].astype(jnp.int32), work_len.astype(jnp.int32)])
    home_tokens = tokens[0].reshape(cap_dev, SLOT, width)
    home_cot = cotangent[0].reshape(cap_dev, SLOT, width)

    def travel(table):
        packs = gather_slots(send_idx, [table], [QCAP // 2] * (SPREAD - 1))
        got = [caption_shift(pack, -(o + 1)) for o, pack in enumerate(packs)]
        return got

    def settle(table, got):
        other = [swap_mp(g, True) for g in got]
        return gather_slots(work_idx, [table] + got + other, [per_core])[0].reshape(rows, width)

    got_tokens = travel(home_tokens)
    image_rows = lax.dynamic_slice_in_dim(tokens[0], c * rows, rows)
    pairs = [(2 * d + k, 2 * (count + d) + k) for d in range(count) for k in range(2)]
    image_here = lax.ppermute(image_rows, ("half", "dp", "mp"), pairs)
    got_cot = travel(home_cot)

    qkv = jnp.transpose(qkv_weight[0], (1, 0, 2))
    cross = jnp.stack([cross_query_matrix, cross_keyval[:, 0], cross_keyval[:, 1]])
    gen_own = jnp.where(is_image, qkv, cross)
    gen_out_own = jnp.where(is_image, out_weight[0], cross_out)
    gen_oth = swap_mp(gen_own)
    gen_out_oth = swap_mp(gen_out_own)
    qkv_oth = swap_mp(qkv, True)
    out_oth = swap_mp(out_weight[0], True)
    up_oth = swap_mp(up_weight[0])
    down_oth = swap_mp(down_weight[0])

    x = settle(home_tokens, got_tokens)
    cot = settle(home_cot, got_cot)
    gains = norm_gains[0]
    gain_cross = cross_gain[None]
    heads_shape = ((6, rows, 128), BF16)
    wide, narrow = ((rows, width), F32), ((rows, width), BF16)
    head_scratch = pltpu.VMEM((6, rows, 128), BF16)
    bias_scratch = pltpu.VMEM((3, GROUP, GROUP), F32)
    a, r, normed, sq, sk, sv, st = call(
        pre_kernel,
        "pre",
        [narrow, wide, narrow, heads_shape, heads_shape, heads_shape, heads_shape],
        [bias_scratch],
        True,
        meta, x, gains, gain_cross, qkv, qkv_oth, out_weight[0], out_oth,
    )
    b = jnp.where(is_image, a, image_here)
    q, k, v, ctx, sums, mixed, ffn_in = call(
        mid_kernel,
        "mid",
        [heads_shape, heads_shape, heads_shape, heads_shape, ((12, 1, rows), F32), wide, narrow],
        [],
        True,
        meta, a, b, r, gains, gen_own, gen_oth, gen_out_own, gen_out_oth,
    )
    ffn_g_oth, acc_out, acc_grad = ffn_call(False, ffn_in, cot, up_oth, down_oth)
    ffn_arrived = swap_mp(ffn_g_oth)
    ffn_g_own, y, gm, gain_ffn = ffn_call(True, ffn_in, cot, up_weight[0], down_weight[0], acc_out, acc_grad, mixed, gains)
    ffn_sum = reduce_dp(ffn_g_own, ffn_arrived)

    g_own, g_oth, da, db = call(
        back_kernel,
        "back",
        [((4, width, width // 2), BF16), ((4, width, width // 2), BF16), wide, wide],
        [head_scratch] * 4,
        True,
        meta, gm, ctx, sums, q, k, v, a, b, gen_own, gen_oth, gen_out_own, gen_out_oth,
    )
    gen_sum = reduce_dp(g_own, swap_mp(g_oth))
    image_part = lax.ppermute(db.astype(BF16), ("half", "dp", "mp"), [(d, s) for s, d in pairs])

    gt, g3_own, g3_oth, gain_two = call(
        post_kernel,
        "post",
        [wide, ((4, width, width // 2), BF16), ((4, width, width // 2), BF16), ((2, width), F32)],
        [bias_scratch] + [head_scratch] * 4 + [pltpu.VMEM((rows, width), F32)],
        True,
        meta, x, gains, gain_cross, gm, da, db, r, normed, sq, sk, sv, st, qkv, qkv_oth, out_weight[0], out_oth,
    )
    cap_sum = reduce_dp(g3_own, swap_mp(g3_oth))
    grad_rows = jnp.where(is_image, gt + image_part.astype(F32), gt).astype(BF16)

    def go_home(values):
        own = values.reshape(per_core, SLOT, width)
        other = swap_mp(own)
        packs = gather_slots(back_idx, [own, other], [QCAP // 2] * (SPREAD - 1))
        got = [caption_shift(pack, o + 1) for o, pack in enumerate(packs)]
        more = [swap_mp(g, True) for g in got]
        return gather_slots(home_idx, [own, other] + got + more, [cap_dev])[0].reshape(row_count, width)

    layer_out = go_home(y)
    grad_tokens = go_home(grad_rows).astype(F32)

    zero = jnp.zeros_like(gain_ffn)
    mine = jnp.concatenate([gain_two[0:1], gain_ffn])
    none = jnp.zeros_like(mine)
    gain_rows = jnp.concatenate(
        [jnp.where(is_image, mine, none), jnp.where(is_image, none, mine), gain_two[1:2]]
    )
    gain_rows = lax.psum(gain_rows, ("half", "dp", "mp"))
    part = width // count
    gain_rows = lax.dynamic_slice_in_dim(gain_rows, me * part, part, axis=1)
    sum_gains = jnp.where(is_image, gain_rows[0:2], gain_rows[2:4])
    sum_cross_gain = gain_rows[4]

    cross_low = gen_sum.astype(BF16)
    cross_arrived = lax.ppermute(cross_low, ("half", "dp", "mp"), [(d, s) for s, d in pairs])
    cross_sum = jnp.where(is_image, cross_arrived, cross_low).astype(F32)
    tower_sum = jnp.where(is_image, gen_sum, cap_sum)
    return (
        layer_out[None],
        grad_tokens[None],
        jnp.transpose(tower_sum[1:4], (1, 0, 2))[None],
        tower_sum[0].T[None],
        ffn_sum[0][None],
        ffn_sum[1].T[None],
        sum_gains[None],
        sum_cross_gain,
        cross_sum[1],
        jnp.stack([cross_sum[2], cross_sum[3]], axis=1),
        cross_sum[0].T,
    )


def solution(mesh):
    placed = (
        P("half", "dp", None),
        P("half", None, None, "mp"),
        P("half", "mp", None),
        P("half", None, "mp"),
        P("half", "mp", None),
        P("half", None, None),
        P(),
        P(None, "mp"),
        P(None, None, "mp"),
        P("mp", None),
        P(),
        P(),
        P("half", "dp", None),
    )
    return jax.shard_map(
        shards,
        mesh=mesh,
        in_specs=placed,
        out_specs=(
            P("half", "dp", None),
            P("half", "dp", None),
            P("half", "dp", None, "mp"),
            P("half", "mp", "dp"),
            P("half", "dp", "mp"),
            P("half", "mp", "dp"),
            P("half", None, "dp"),
            P("dp"),
            P("dp", "mp"),
            P("dp", None, "mp"),
            P("mp", "dp"),
        ),
        check_vma=False,
    )
```

```python
import functools

import jax
import jax.numpy as jnp
from jax import lax
from jax.experimental import pallas as pl
from jax.experimental.pallas import tpu as pltpu
from jax.sharding import PartitionSpec as P

HEAD = 64
PATCH = 576
SLOT = 64
SPREAD = 4
IMG_DEV = 2
QCAP = 6
CAPS = 8

EPS = 1e-06
NEG = -1e30
SCALE = HEAD**-0.5

F32 = jnp.float32
BF16 = jnp.bfloat16
VMEM = pl.BlockSpec(memory_space=pltpu.VMEM)
SMEM = pl.BlockSpec(memory_space=pltpu.SMEM)
ANY = pl.BlockSpec(memory_space=pl.ANY)
LIMIT = 56 * 1024 * 1024


def dot(a, b):
    return lax.dot_general(a, b, (((1,), (0,)), ((), ())), preferred_element_type=F32)


def dot_nt(a, b):
    return lax.dot_general(a, b, (((1,), (1,)), ((), ())), preferred_element_type=F32)


def dot_tn(a, b):
    return lax.dot_general(a, b, (((0,), (0,)), ((), ())), preferred_element_type=F32)


def norm_stats(v):
    mean = jnp.mean(v, axis=-1, keepdims=True)
    centred = v - mean
    rstd = lax.rsqrt(jnp.mean(centred * centred, axis=-1, keepdims=True) + EPS)
    return centred * rstd, rstd


def norm_rows(v, gain):
    return norm_stats(v)[0] * gain


def norm_back(v, gain, dn):
    x_hat, rstd = norm_stats(v)
    dg = dn * gain
    m1 = jnp.mean(dg, axis=-1, keepdims=True)
    m2 = jnp.mean(dg * x_hat, axis=-1, keepdims=True)
    return (dg - m1 - x_hat * m2) * rstd, jnp.sum(dn * x_hat, axis=0, keepdims=True)


def head_masks():
    lane = lax.broadcasted_iota(jnp.int32, (1, 2 * HEAD), 1)
    first = (lane < HEAD).astype(F32)
    return first.astype(BF16), (1.0 - first).astype(BF16)


def three(ref, half):
    return jnp.concatenate([ref[3 * half], ref[3 * half + 1], ref[3 * half + 2]], axis=1)


def attend(q, k, v, masks, bias):
    v_t = v.T
    outs, sums = [], []
    for h in range(2):
        s = dot_nt(k, q * masks[h])
        if bias is not None:
            s = s + bias
        top = jnp.max(s, axis=0, keepdims=True)
        e = jnp.exp(s - top)
        total = jnp.sum(e, axis=0, keepdims=True)
        p = (e * (1.0 / total)).astype(BF16)
        outs.append(dot(v_t[h * HEAD : (h + 1) * HEAD], p))
        sums.append(top + jnp.log(total))
    return jnp.concatenate(outs, axis=0).T.astype(BF16), sums


def attend_back(q, k, v, do, masks, bias, sums):
    k_t = k.T
    dqs = []
    dk = dv = None
    for h in range(2):
        qh = q * masks[h]
        doh = do * masks[h]
        s = dot_nt(k, qh)
        if bias is not None:
            s = s + bias
        if sums is None:
            e = jnp.exp(s - jnp.max(s, axis=0, keepdims=True))
            p = e * (1.0 / jnp.sum(e, axis=0, keepdims=True))
        else:
            p = jnp.exp(s - sums[h])
        dp = dot_nt(v, doh)
        delta = jnp.sum(p * dp, axis=0, keepdims=True)
        ds = (p * (dp - delta)).astype(BF16)
        dv_h = dot(p.astype(BF16), doh)
        dk_h = dot(ds, qh)
        dv = dv_h if dv is None else dv + dv_h
        dk = dk_h if dk is None else dk + dk_h
        dqs.append(dot(k_t[h * HEAD : (h + 1) * HEAD], ds))
    dq = (jnp.concatenate(dqs, axis=0) * SCALE).T
    return dq.astype(BF16), dk.astype(BF16), dv.astype(BF16)


GROUP = 3 * SLOT


def caption_bias(meta, bias):
    key = lax.broadcasted_iota(jnp.int32, (GROUP, GROUP), 0)
    query = lax.broadcasted_iota(jnp.int32, (GROUP, GROUP), 1)
    key_slot, key_pos = key >> 6, key & 63
    same = (key_slot == (query >> 6)) & (key_pos <= (query & 63))
    for g in range(3):
        limit = jnp.where(
            key_slot == 0,
            meta[1 + 3 * g],
            jnp.where(key_slot == 1, meta[2 + 3 * g], meta[3 + 3 * g]),
        )
        keep = same & ((key_pos < limit) | (key_pos == 0))
        bias[g] = jnp.where(keep, 0.0, NEG)


def pre_kernel(meta, x, gain, gain_cross, w_own, w_oth, o_own, o_oth, a_ref, r_ref, n_ref, q_ref, k_ref, v_ref, t_ref, bias):
    source = x[...].astype(F32)
    normed = norm_rows(source, gain[0:1, :]).astype(BF16)
    n_ref[...] = normed

    @pl.when(meta[0] == 0)
    def _():
        a_ref[...] = normed
        r_ref[...] = source

    @pl.when(meta[0] == 1)
    def _():
        caption_bias(meta, bias)
        for half, w in ((0, w_own), (1, w_oth)):
            for j, ref in enumerate((q_ref, k_ref, v_ref)):
                rows = dot(n_ref[...], w[j]).astype(BF16)
                if j == 0:
                    rows = rows * SCALE
                for p in range(3):
                    ref[3 * half + p] = rows[:, p * 128 : (p + 1) * 128]
        masks = head_masks()

        @pl.loop(0, 6)
        def _(p):
            for g in range(3):
                at = slice(g * GROUP, (g + 1) * GROUP)
                out, unused = attend(q_ref[p, at], k_ref[p, at], v_ref[p, at], masks, bias[g])
                t_ref[p, at] = out

        hidden = x[...].astype(F32) + dot(three(t_ref, 0), o_own[...]) + dot(three(t_ref, 1), o_oth[...])
        r_ref[...] = hidden
        a_ref[...] = norm_rows(hidden, gain_cross[...]).astype(BF16)


def mid_kernel(meta, a_ref, b_ref, r_ref, gain, w_own, w_oth, o_own, o_oth, q_ref, k_ref, v_ref, c_ref, s_ref, m_ref, f_ref):
    rows_in = a_ref.shape[0]
    for half, w in ((0, w_own), (1, w_oth)):
        for j, (ref, src) in enumerate(((q_ref, a_ref), (k_ref, b_ref), (v_ref, b_ref))):
            rows = dot(src[...], w[j]).astype(BF16)
            if j == 0:
                rows = rows * SCALE
            for p in range(3):
                ref[3 * half + p] = rows[:, p * 128 : (p + 1) * 128]
    masks = head_masks()

    @pl.loop(0, 6)
    def _(p):
        out, sums = attend(q_ref[p], k_ref[p], v_ref[p], masks, None)
        c_ref[p] = out
        s_ref[2 * p] = sums[0]
        s_ref[2 * p + 1] = sums[1]

    @pl.when(meta[0] == 1)
    def _():
        for p in range(6):
            c_ref[p, CAPS * SLOT : rows_in] = jnp.zeros((rows_in - CAPS * SLOT, 128), BF16)

    mixed = r_ref[...] + dot(three(c_ref, 0), o_own[...]) + dot(three(c_ref, 1), o_oth[...])
    m_ref[...] = mixed
    f_ref[...] = norm_rows(mixed, gain[1:2, :]).astype(BF16)


def ffn_kernel(last, f_ref, cot, up, down, *rest):
    if last:
        out_in, grad_in, mixed, gain, g_ref, y_ref, gm_ref, gg_ref, acc_out, acc_grad = rest
    else:
        g_ref, acc_out, acc_grad = rest
    step = pl.program_id(0)

    @pl.when(step == 0)
    def _():
        if last:
            acc_out[...] = out_in[...]
            acc_grad[...] = grad_in[...]
        else:
            acc_out[...] = jnp.zeros_like(acc_out)
            acc_grad[...] = jnp.zeros_like(acc_grad)

    upward = dot(f_ref[...], up[...])
    phi = 0.5 * (1.0 + lax.erf(upward * (0.5**0.5)))
    active = (upward * phi).astype(BF16)
    slope = phi + upward * (jnp.exp(-0.5 * upward * upward) * 0.3989422804014327)
    grad_active = dot_nt(cot[...], down[...])
    grad_upward = (grad_active * slope).astype(BF16)
    acc_out[...] += dot(active, down[...])
    g_ref[1] = dot_tn(cot[...], active).astype(BF16)
    g_ref[0] = dot_tn(f_ref[...], grad_upward).astype(BF16)
    acc_grad[...] += dot_nt(grad_upward, up[...])
    if last:

        @pl.when(step == pl.num_programs(0) - 1)
        def _():
            y_ref[...] = (mixed[...] + acc_out[...]).astype(BF16)
            back, gain_grad = norm_back(mixed[...], gain[1:2, :], acc_grad[...])
            gm_ref[...] = cot[...].astype(F32) + back
            gg_ref[...] = gain_grad


def back_kernel(meta, gm_ref, c_ref, s_ref, q_ref, k_ref, v_ref, a_ref, b_ref, w_own, w_oth, o_own, o_oth, g_own, g_oth, da_ref, db_ref, do_ref, dq_ref, dk_ref, dv_ref):
    rows_in = a_ref.shape[0]
    low = gm_ref[...].astype(BF16)
    for half, o, g in ((0, o_own, g_own), (1, o_oth, g_oth)):
        g[0] = dot_tn(low, three(c_ref, half)).astype(BF16)
        rows = dot_nt(low, o[...]).astype(BF16)
        for p in range(3):
            do_ref[3 * half + p] = rows[:, p * 128 : (p + 1) * 128]

    @pl.when(meta[0] == 1)
    def _():
        for p in range(6):
            do_ref[p, CAPS * SLOT : rows_in] = jnp.zeros((rows_in - CAPS * SLOT, 128), BF16)

    masks = head_masks()

    @pl.loop(0, 6)
    def _(p):
        sums = (s_ref[2 * p], s_ref[2 * p + 1])
        dq, dk, dv = attend_back(q_ref[p], k_ref[p], v_ref[p], do_ref[p], masks, None, sums)
        dq_ref[p] = dq
        dk_ref[p] = dk
        dv_ref[p] = dv

    for half, w, g in ((0, w_own, g_own), (1, w_oth, g_oth)):
        dq, dk, dv = three(dq_ref, half), three(dk_ref, half), three(dv_ref, half)
        g[1] = dot_tn(a_ref[...], dq).astype(BF16)
        g[2] = dot_tn(b_ref[...], dk).astype(BF16)
        g[3] = dot_tn(b_ref[...], dv).astype(BF16)
        part_a = dot_nt(dq, w[0])
        part_b = dot_nt(dk, w[1]) + dot_nt(dv, w[2])
        if half == 0:
            da_ref[...] = part_a
            db_ref[...] = part_b
        else:
            da_ref[...] += part_a
            db_ref[...] += part_b


def post_kernel(meta, x, gain, gain_cross, gm_ref, da_ref, db_ref, r_ref, n_ref, q_ref, k_ref, v_ref, t_ref, w_own, w_oth, o_own, o_oth, gt_ref, g_own, g_oth, gg_ref, bias, do_ref, dq_ref, dk_ref, dv_ref, gh_ref):
    @pl.when(meta[0] == 0)
    def _():
        back, gain_grad = norm_back(x[...].astype(F32), gain[0:1, :], da_ref[...] + db_ref[...])
        gt_ref[...] = gm_ref[...] + back
        gg_ref[0:1, :] = gain_grad
        gg_ref[1:2, :] = jnp.zeros_like(gain_grad)

    @pl.when(meta[0] == 1)
    def _():
        caption_bias(meta, bias)
        back, gain_grad = norm_back(r_ref[...], gain_cross[...], da_ref[...])
        gg_ref[1:2, :] = gain_grad
        gh_ref[...] = gm_ref[...] + back
        low = gh_ref[...].astype(BF16)
        for half, o, g in ((0, o_own, g_own), (1, o_oth, g_oth)):
            g[0] = dot_tn(low, three(t_ref, half)).astype(BF16)
            rows = dot_nt(low, o[...]).astype(BF16)
            for p in range(3):
                do_ref[3 * half + p] = rows[:, p * 128 : (p + 1) * 128]
        masks = head_masks()

        @pl.loop(0, 6)
        def _(p):
            for g in range(3):
                at = slice(g * GROUP, (g + 1) * GROUP)
                dq, dk, dv = attend_back(
                    q_ref[p, at], k_ref[p, at], v_ref[p, at], do_ref[p, at], masks, bias[g], None
                )
                dq_ref[p, at] = dq
                dk_ref[p, at] = dk
                dv_ref[p, at] = dv

        total = None
        for half, w, g in ((0, w_own, g_own), (1, w_oth, g_oth)):
            for j, ref in enumerate((dq_ref, dk_ref, dv_ref)):
                rows = three(ref, half)
                g[1 + j] = dot_tn(n_ref[...], rows).astype(BF16)
                part = dot_nt(rows, w[j])
                total = part if total is None else total + part
        back, gain_grad = norm_back(x[...].astype(F32), gain[0:1, :], total)
        gt_ref[...] = gh_ref[...] + back
        gg_ref[0:1, :] = gain_grad


def gather_kernel(table_sizes, out_sizes, idx, *refs):
    tables = refs[: len(table_sizes)]
    outs = refs[len(table_sizes) : len(table_sizes) + len(out_sizes)]
    sems = refs[-1]
    at = 0
    waits = []
    for out, size in zip(outs, out_sizes):
        for row in range(size):
            code = idx[at]
            base = 0
            for table, count in zip(tables, table_sizes):

                @pl.when((code >= base) & (code < base + count))
                def _():
                    pltpu.make_async_copy(table.at[code - base], out.at[row], sems.at[at]).start()

                base += count
            waits.append(pltpu.make_async_copy(tables[0].at[0], out.at[row], sems.at[at]))
            at += 1
    for wait in waits:
        wait.wait()


def gather_slots(idx, tables, out_sizes):
    sizes = tuple(table.shape[0] for table in tables)
    block = tables[0].shape[1:]
    return pl.pallas_call(
        functools.partial(gather_kernel, sizes, tuple(out_sizes)),
        out_shape=[jax.ShapeDtypeStruct((n,) + block, tables[0].dtype) for n in out_sizes],
        in_specs=[SMEM] + [ANY] * len(tables),
        out_specs=[ANY] * len(out_sizes),
        scratch_shapes=[pltpu.SemaphoreType.DMA((sum(out_sizes),))],
        name="gather_slots",
    )(idx, *tables)


def call(kernel, name, outs, scratch, smem_first, *args):
    return pl.pallas_call(
        kernel,
        out_shape=[jax.ShapeDtypeStruct(shape, dtype) for shape, dtype in outs],
        in_specs=([SMEM] if smem_first else []) + [VMEM] * (len(args) - int(smem_first)),
        out_specs=[VMEM] * len(outs),
        scratch_shapes=scratch,
        compiler_params=pltpu.CompilerParams(vmem_limit_bytes=LIMIT),
        name=name,
    )(*args)


def ffn_call(last, ffn_in, cot, up, down, *extra):
    rows, width = ffn_in.shape
    hidden = up.shape[1]
    chunk = hidden // 3
    whole = pl.BlockSpec((rows, width), lambda j: (0, 0))
    in_specs = [
        whole,
        whole,
        pl.BlockSpec((width, chunk), lambda j: (0, j)),
        pl.BlockSpec((chunk, width), lambda j: (j, 0)),
    ]
    g_spec = pl.BlockSpec((2, width, chunk), lambda j: (0, 0, j))
    g_shape = jax.ShapeDtypeStruct((2, width, hidden), BF16)
    wide = jax.ShapeDtypeStruct((rows, width), F32)
    if last:
        in_specs += [whole, whole, whole, pl.BlockSpec(extra[3].shape, lambda j: (0, 0))]
        out_shape = [g_shape, jax.ShapeDtypeStruct((rows, width), BF16), wide, jax.ShapeDtypeStruct((1, width), F32)]
        out_specs = [g_spec, whole, whole, pl.BlockSpec((1, width), lambda j: (0, 0))]
        scratch = [pltpu.VMEM((rows, width), F32)] * 2
    else:
        out_shape = [g_shape, wide, wide]
        out_specs = [g_spec, whole, whole]
        scratch = []
    return pl.pallas_call(
        functools.partial(ffn_kernel, last),
        grid=(3,),
        out_shape=out_shape,
        in_specs=in_specs,
        out_specs=out_specs,
        scratch_shapes=scratch,
        compiler_params=pltpu.CompilerParams(vmem_limit_bytes=LIMIT),
        name="ffn_own" if last else "ffn_other",
    )(ffn_in, cot, up, down, *extra)


MESH = pl.DeviceIdType.MESH
STEPS = SPREAD - 1
PACK = QCAP // 2


class Links:
    def __init__(self, send_sems, recv_sems):
        self.send, self.recv, self.used = send_sems, recv_sems, 0

    def copy(self, src, dst, device):
        at = self.used
        self.used += 1
        return pltpu.make_async_remote_copy(
            src_ref=src,
            dst_ref=dst,
            send_sem=self.send.at[at],
            recv_sem=self.recv.at[at],
            device_id=device,
            device_id_type=MESH,
        )


def place(count):
    side, me, c = lax.axis_index("half"), lax.axis_index("dp"), lax.axis_index("mp")
    return side, me, c, lambda k: (side, lax.rem(me + k + count, count), c)


def greet(both, captions, side):
    barrier = pltpu.get_barrier_semaphore()
    for device in both:
        pl.semaphore_signal(barrier, inc=1, device_id=device, device_id_type=MESH)

    @pl.when(side == 0)
    def _():
        pl.semaphore_wait(barrier, len(both))

    @pl.when(side == 1)
    def _():
        for device in captions:
            pl.semaphore_signal(barrier, inc=1, device_id=device, device_id_type=MESH)
        pl.semaphore_wait(barrier, len(both) + len(captions))


def choose(code, near, far):
    split = near.shape[0]
    a = near[jnp.minimum(code, split - 1)]
    b = far[jnp.maximum(code - split, 0)]
    return jnp.where(code < split, a, b)


def route_kernel(count, send_idx, work_idx, home_t, home_c, qkv, out_w, gen, gen_out, up, down, x, cot, image, qkv_o, out_o, gen_o, gen_out_o, up_o, down_o, near_t, near_c, far_t, far_c, pack_t, pack_c, send_sems, recv_sems, local_sems):
    side, me, c, along = place(count)
    twin = (side, me, 1 - c)
    across = (1 - side, me, c)
    links = Links(send_sems, recv_sems)
    slots = home_t.shape[0]
    half = slots // 2
    loads = [
        pltpu.make_async_copy(home_t, near_t, local_sems.at[0]),
        pltpu.make_async_copy(home_c, near_c, local_sems.at[1]),
    ]
    for load in loads:
        load.start()
    greet([twin, across], [along(k) for k in (-3, -2, -1, 1, 2, 3)], side)

    first = [links.copy(gen, gen_o, twin), links.copy(gen_out, gen_out_o, twin)]
    for copy in first:
        copy.start()
    picture = links.copy(home_t.at[pl.ds(c * half, half)], image, across)
    late = [links.copy(up, up_o, twin), links.copy(down, down_o, twin)]
    own = [links.copy(qkv, qkv_o, twin), links.copy(out_w, out_o, twin)]
    hops = []
    for far, pack in ((far_t, pack_t), (far_c, pack_c)):
        for o in range(STEPS):
            there = far.at[pl.ds(PACK * o, PACK)]
            hops.append(
                (
                    links.copy(pack.at[o], there, along(-o - 1)),
                    links.copy(there, far.at[pl.ds(PACK * (STEPS + o), PACK)], twin),
                )
            )
    for load in loads:
        load.wait()

    @pl.when(side == 0)
    def _():
        picture.start()
        for copy in late:
            copy.start()

    @pl.when(side == 1)
    def _():
        for which, (table, pack) in enumerate(((near_t, pack_t), (near_c, pack_c))):
            for o in range(STEPS):
                for j in range(PACK):
                    pack[o, j] = table[send_idx[PACK * o + j]]
                hops[STEPS * which + o][0].start()
        for copy in own:
            copy.start()
        for hop, forward in hops[:STEPS]:
            hop.wait_recv()
            forward.start()
        for copy in late:
            copy.start()
        for hop, forward in hops[STEPS:]:
            hop.wait_recv()
            forward.start()
        for hop, forward in hops:
            hop.wait_send()
            forward.wait()
        for copy in own:
            copy.wait()
        picture.wait_recv()

    for p in range(half):
        x[p] = choose(work_idx[p], near_t, far_t)
        cot[p] = choose(work_idx[p], near_c, far_c)

    @pl.when(side == 0)
    def _():
        picture.wait_send()

    for copy in first + late:
        copy.wait()


def route_in(count, send_idx, work_idx, home_t, home_c, qkv, out_w, gen, gen_out, up, down):
    slots = home_t.shape[0]
    block = home_t.shape[1:]
    half = slots // 2

    def like(value):
        return jax.ShapeDtypeStruct(value.shape, value.dtype)

    weights = (qkv, out_w, gen, gen_out, up, down)
    rows = jax.ShapeDtypeStruct((half,) + block, BF16)
    near = pltpu.VMEM((slots,) + block, BF16)
    far = pltpu.VMEM((2 * STEPS * PACK,) + block, BF16)
    pack = pltpu.VMEM((STEPS, PACK) + block, BF16)
    return pl.pallas_call(
        functools.partial(route_kernel, count),
        out_shape=[rows, rows, rows] + [like(w) for w in weights],
        in_specs=[SMEM, SMEM] + [ANY] * 8,
        out_specs=[VMEM, VMEM] + [ANY] * 7,
        scratch_shapes=[near, near, far, far, pack, pack]
        + [pltpu.SemaphoreType.DMA((20,)), pltpu.SemaphoreType.DMA((20,)), pltpu.SemaphoreType.DMA((2,))],
        compiler_params=pltpu.CompilerParams(vmem_limit_bytes=LIMIT, collective_id=0, has_side_effects=True),
        name="route_in",
    )(send_idx, work_idx, home_t, home_c, *weights)


class Job:
    def __init__(self, links, spot, own, other, m, xs, xr, z1s, z1r, z2s, z2r):
        self.own, self.m, self.xs, self.xr = own, m, xs, xr
        self.z1s, self.z1r, self.z2s, self.z2r = z1s, z1r, z2s, z2r
        side, me, c = spot
        self.rows = own.shape[1] // 8
        self.bx, self.b1, self.b2 = me % 2, (me // 2) % 2, me // 4
        flip_x, flip_1, flip_2 = 1 - 2 * self.bx, 2 - 4 * self.b1, 4 - 8 * self.b2
        self.mp = links.copy(other, m, (side, me, 1 - c))
        self.hop_x = links.copy(xs, xr, (side, me + flip_x, c))
        self.hop_1 = links.copy(z1s, z1r, (side, me + flip_1, c))
        self.hop_2 = links.copy(z2s, z2r, (side, me + flip_2, c))

    def at(self, zz, bx):
        return pl.ds(pl.multiple_of((2 * zz + bx) * self.rows, self.rows), self.rows)

    def base(self, i, zz, bx):
        at = self.at(zz, bx)
        return self.own[i, at, :].astype(F32) + self.m[i, at, :].astype(F32)

    def step_mp(self):
        self.mp.start()

    def step_x(self):
        self.mp.wait_recv()
        for i in range(self.own.shape[0]):
            for zz in range(4):
                self.xs[i, zz] = self.base(i, zz, 1 - self.bx).astype(BF16)
        self.hop_x.start()

    def step_1(self):
        self.hop_x.wait_recv()
        for i in range(self.own.shape[0]):
            for b2 in range(2):
                zz = 2 * b2 + 1 - self.b1
                total = self.base(i, zz, self.bx) + self.xr[i, zz].astype(F32)
                self.z1s[i, b2] = total.astype(BF16)
        self.hop_1.start()

    def last(self, i, b2):
        zz = 2 * b2 + self.b1
        total = self.base(i, zz, self.bx) + self.xr[i, zz].astype(F32)
        return total + self.z1r[i, b2].astype(F32)

    def step_2(self):
        self.hop_1.wait_recv()
        for i in range(self.own.shape[0]):
            self.z2s[i] = self.last(i, 1 - self.b2).astype(BF16)
        self.hop_2.start()

    def total(self, i):
        return self.last(i, self.b2) + self.z2r[i].astype(F32)

    def finish(self):
        self.hop_2.wait_recv()

    def drain(self):
        for copy in (self.mp, self.hop_x, self.hop_1, self.hop_2):
            copy.wait_send()


def job_scratch(lead, rows, cols):
    part = rows // 8
    return [pltpu.VMEM((lead, rows, cols), BF16)] + [
        pltpu.VMEM((lead,) + n + (part, cols), BF16) for n in ((4,), (4,), (2,), (2,), (), ())
    ]


def comm_kernel(count, back_idx, home_idx, f_own, f_oth, g_own, g_oth, t_own, t_oth, y_own, r_own, gains, ffn_out, tower_out, cross_out, y_out, r_out, gain_out, *rest):
    jobs_scratch = [rest[8 * k : 8 * k + 7] + (rest[8 * k + 7],) for k in range(5)]
    rest = rest[40:]
    near_y, near_r, far_y, far_r, pack_y, pack_r, cross_low, cross_got, gain_s, gain_r, send_sems, recv_sems, local_sems = rest
    side, me, c, along = place(count)
    twin, across = (side, me, 1 - c), (1 - side, me, c)
    links = Links(send_sems, recv_sems)
    bx, b1, b2 = me % 2, (me // 2) % 2, me // 4
    flips = [(side, me + 1 - 2 * bx, c), (side, me + 2 - 4 * b1, c), (side, me + 4 - 8 * b2, c)]
    chunk = f_own.shape[2] // 3
    half = y_own.shape[0]
    slots = 2 * half

    loads, jobs = [], []
    for k in range(5):
        own = jobs_scratch[k][7]
        if k < 3:
            at = pl.ds(k * chunk, chunk)
            source, other = f_own.at[:, :, at], f_oth.at[:, :, at]
        else:
            source, other = (g_own, g_oth) if k == 3 else (t_own, t_oth)
        loads.append(pltpu.make_async_copy(source, own, local_sems.at[k]))
        jobs.append(Job(links, (side, me, c), own, other, *jobs_scratch[k][:7]))
    loads.append(pltpu.make_async_copy(y_own, near_y.at[pl.ds(0, half)], local_sems.at[5]))
    loads.append(pltpu.make_async_copy(r_own, near_r.at[pl.ds(0, half)], local_sems.at[6]))
    for load in loads:
        load.start()
    swaps = [
        links.copy(own, table.at[pl.ds(half, half)], twin) for own, table in ((y_own, near_y), (r_own, near_r))
    ]
    hops = []
    for far, pack in ((far_y, pack_y), (far_r, pack_r)):
        for o in range(STEPS):
            there = far.at[pl.ds(PACK * o, PACK)]
            hops.append(
                (
                    links.copy(pack.at[o], there, along(o + 1)),
                    links.copy(there, far.at[pl.ds(PACK * (STEPS + o), PACK)], twin),
                )
            )
    gain_copies = [links.copy(gain_s.at[k], gain_r.at[k], device) for k, device in enumerate([twin] + flips + [across])]
    cross_copy = links.copy(cross_low, cross_got, across)
    greet([twin, across] + flips, [along(k) for k in (-3, -2, -1, 1, 2, 3)], side)

    for swap in swaps:
        swap.start()
    for job in jobs[:4]:
        job.step_mp()

    @pl.when(side == 1)
    def _():
        jobs[4].step_mp()

    gain_s[0] = gains[...]
    gain_copies[0].start()
    for load in loads:
        load.wait()
    for job in jobs[:3]:
        job.step_x()

    def gain_step(k):
        gain_copies[k].wait_recv()
        gain_s[k + 1] = gain_s[k] + gain_r[k]
        if k < 3:
            gain_copies[k + 1].start()

    gain_step(0)
    for swap in swaps:
        swap.wait_recv()

    @pl.when(side == 1)
    def _():
        for which, (table, pack) in enumerate(((near_y, pack_y), (near_r, pack_r))):
            for o in range(STEPS):
                for j in range(PACK):
                    pack[o, j] = table[back_idx[PACK * o + j]]
                hops[STEPS * which + o][0].start()

    jobs[3].step_x()
    gain_step(1)

    @pl.when(side == 1)
    def _():
        jobs[4].step_x()
        for hop, forward in hops:
            hop.wait_recv()
            forward.start()

    gain_step(2)
    jobs[0].step_1()
    jobs[1].step_1()
    jobs[2].step_1()
    jobs[0].step_2()
    jobs[3].step_1()
    jobs[1].step_2()
    jobs[2].step_2()

    @pl.when(side == 1)
    def _():
        jobs[4].step_1()

    jobs[3].step_2()

    @pl.when(side == 1)
    def _():
        jobs[4].step_2()

    gain_step(3)

    @pl.when(side == 1)
    def _():
        gain_copies[4].start()

    for k in range(3):
        jobs[k].finish()
        for i in range(2):
            ffn_out[i, :, k * chunk : (k + 1) * chunk] = jobs[k].total(i)
    jobs[3].finish()

    @pl.when(side == 1)
    def _():
        for i in range(4):
            low = jobs[3].total(i).astype(BF16)
            cross_low[i] = low
            cross_out[i] = low.astype(F32)
        cross_copy.start()
        jobs[4].finish()
        for i in range(4):
            tower_out[i] = jobs[4].total(i)
        gain_out[...] = gain_s[4]
        for hop, forward in hops:
            hop.wait_send()
            forward.wait()

    @pl.when(side == 0)
    def _():
        for i in range(4):
            tower_out[i] = jobs[3].total(i)

    for s in range(slots):
        y_out[s] = choose(home_idx[s], near_y, far_y)
        r_out[s] = choose(home_idx[s], near_r, far_r).astype(F32)

    @pl.when(side == 0)
    def _():
        cross_copy.wait_recv()
        for i in range(4):
            cross_out[i] = cross_got[i].astype(F32)
        gain_copies[4].wait_recv()
        gain_out[...] = gain_s[4]
        gain_out[2:3, :] = gain_r[4, 2:3, :]

    @pl.when(side == 1)
    def _():
        cross_copy.wait_send()
        gain_copies[4].wait_send()
        jobs[4].drain()

    for copy in gain_copies[:4] + swaps:
        copy.wait_send()
    for job in jobs[:4]:
        job.drain()


def comm(count, back_idx, home_idx, f_own, f_oth, g_own, g_oth, t_own, t_oth, y_own, r_own, gains):
    lead, width, hidden = f_own.shape
    part = width // count
    half, block = y_own.shape[0], y_own.shape[1:]
    slots = 2 * half
    scratch = []
    for k in range(5):
        shape = (2, width, hidden // 3) if k < 3 else g_own.shape
        scratch += job_scratch(*shape) + [pltpu.VMEM(shape, BF16)]
    near = pltpu.VMEM((slots,) + block, BF16)
    far = pltpu.VMEM((2 * STEPS * PACK,) + block, BF16)
    pack = pltpu.VMEM((STEPS, PACK) + block, BF16)
    small = (4, part, g_own.shape[2])
    scratch += [near, near, far, far, pack, pack, pltpu.VMEM(small, BF16), pltpu.VMEM(small, BF16)]
    scratch += [pltpu.VMEM((5,) + gains.shape, F32), pltpu.VMEM((5,) + gains.shape, F32)]
    scratch += [pltpu.SemaphoreType.DMA((40,)), pltpu.SemaphoreType.DMA((40,)), pltpu.SemaphoreType.DMA((7,))]
    shapes = [
        ((lead, part, hidden), F32),
        (small, F32),
        (small, F32),
        ((slots,) + block, BF16),
        ((slots,) + block, F32),
        (gains.shape, F32),
    ]
    return pl.pallas_call(
        functools.partial(comm_kernel, count),
        out_shape=[jax.ShapeDtypeStruct(*shape) for shape in shapes],
        in_specs=[SMEM, SMEM] + [ANY] * 8 + [VMEM],
        out_specs=[VMEM] * 6,
        scratch_shapes=scratch,
        compiler_params=pltpu.CompilerParams(vmem_limit_bytes=60 * 1024 * 1024, collective_id=1, has_side_effects=True),
        name="comm",
    )(back_idx, home_idx, f_own, f_oth, g_own, g_oth, t_own, t_oth, y_own, r_own, gains)


def swap_mp(value, captions_only=False):
    if not captions_only:
        return lax.ppermute(value, "mp", [(0, 1), (1, 0)])
    count = lax.axis_size("dp")
    pairs = [((count + d) * 2 + c, (count + d) * 2 + 1 - c) for d in range(count) for c in range(2)]
    return lax.ppermute(value, ("half", "dp", "mp"), pairs)


def caption_shift(value, steps):
    count = lax.axis_size("dp")
    pairs = [
        ((count + d) * 2 + c, (count + (d + steps) % count) * 2 + c) for d in range(count) for c in range(2)
    ]
    return lax.ppermute(value, ("half", "dp", "mp"), pairs)


def reduce_dp(own, arrived):
    count = lax.axis_size("dp")
    me = lax.axis_index("dp")
    lead, rows, cols = own.shape
    bits = count.bit_length() - 1
    shape = (lead,) + (2,) * bits + (rows // count, cols)
    kept, got = own.reshape(shape), arrived.reshape(shape)
    for bit in range(bits):
        axis = bits - bit
        mine = (me >> bit) & 1

        def part(value, which):
            return lax.dynamic_index_in_dim(value, which, axis, keepdims=False).astype(F32)

        send = (part(kept, 1 - mine) + part(got, 1 - mine)).astype(BF16)
        kept = part(kept, mine) + part(got, mine)
        got = lax.ppermute(send, "dp", [(d, d ^ (1 << bit)) for d in range(count)])
        if bit < bits - 1:
            continue
    return kept + got.astype(F32)


def route_tables(slot_image, slot_length, me, c, side, cap_dev):
    total = slot_image.shape[0]
    count = total // cap_dev
    slot = jnp.arange(total)
    home = slot // cap_dev
    filled = slot_length > 0
    image = slot_image
    dest = image // IMG_DEV
    offset = jnp.where(filled, (home - dest) % count, SPREAD)
    core = image % IMG_DEV
    before = slot[None, :] < slot[:, None]
    same_home = home[None, :] == home[:, None]
    same_offset = offset[None, :] == offset[:, None]
    rank = jnp.sum((before & same_home & same_offset).astype(jnp.int32), axis=1)
    place = jnp.sum(
        (before & filled[None, :] & (image[None, :] == image[:, None])).astype(jnp.int32), axis=1
    )
    half_cap = QCAP // 2
    local = slot % cap_dev
    pack_core, pack_row = rank // half_cap, rank % half_cap
    seats = jnp.arange(half_cap)

    def pick(match, code):
        return jnp.sum(jnp.where(match, code[None, :], 0), axis=1)

    offs = jnp.repeat(jnp.arange(1, SPREAD), half_cap)
    rows = jnp.tile(seats, SPREAD - 1)
    mine = (offset[None, :] == offs[:, None]) & (pack_core[None, :] == c) & (pack_row[None, :] == rows[:, None])
    send_idx = pick(mine & (home[None, :] == me), local)
    per_core = cap_dev // 2
    arrived_code = cap_dev + jnp.where(pack_core == c, 0, 9) + (offset - 1) * half_cap + pack_row
    seat = jnp.arange(per_core)
    named = filled & (image == me * IMG_DEV + c)
    hit = jnp.where(
        (seat < CAPS)[:, None],
        named[None, :] & (place[None, :] == seat[:, None]),
        ((~filled) & (home == me) & (rank == c))[None, :],
    )
    work_idx = pick(hit, jnp.where(offset % SPREAD == 0, local, arrived_code))
    work_len = pick(hit, slot_length)
    work_idx = jnp.where(side == 0, c * per_core + seat, work_idx)
    at_core = jnp.where(core == c, 0, per_core) + place
    back_idx = pick(mine & (home[None, :] == (me + offs[:, None]) % count), at_core)
    here = lax.dynamic_slice_in_dim(
        jnp.where(
            filled,
            jnp.where(offset == 0, at_core, cap_dev + jnp.where(pack_core == c, 0, 9) + (offset - 1) * half_cap + pack_row),
            jnp.where(rank == c, 0, per_core) + per_core - 1,
        ),
        me * cap_dev,
        cap_dev,
    )
    spot = jnp.arange(cap_dev)
    home_idx = jnp.where(side == 0, jnp.where(spot // per_core == c, 0, per_core) + spot % per_core, here)
    return send_idx, work_idx, work_len, back_idx, home_idx


def shards(
    tokens,
    qkv_weight,
    out_weight,
    up_weight,
    down_weight,
    norm_gains,
    cross_gain,
    cross_query_matrix,
    cross_keyval,
    cross_out,
    slot_image,
    slot_length,
    cotangent,
):
    count = lax.axis_size("dp")
    side = lax.axis_index("half")
    me = lax.axis_index("dp")
    c = lax.axis_index("mp")
    row_count, width = tokens.shape[1:]
    cap_dev = row_count // SLOT
    per_core = cap_dev // 2
    rows = row_count // 2
    is_image = side == 0

    send_idx, work_idx, work_len, back_idx, home_idx = route_tables(
        slot_image, slot_length, me, c, side, cap_dev
    )
    meta = jnp.concatenate([side[None].astype(jnp.int32), work_len.astype(jnp.int32)])
    home_tokens = tokens[0].reshape(cap_dev, SLOT, width)
    home_cot = cotangent[0].reshape(cap_dev, SLOT, width)

    def travel(table):
        packs = gather_slots(send_idx, [table], [QCAP // 2] * (SPREAD - 1))
        got = [caption_shift(pack, -(o + 1)) for o, pack in enumerate(packs)]
        return got

    def settle(table, got):
        other = [swap_mp(g, True) for g in got]
        return gather_slots(work_idx, [table] + got + other, [per_core])[0].reshape(rows, width)

    fused = count == 8 and width % (count * 32) == 0
    pairs = [(2 * d + k, 2 * (count + d) + k) for d in range(count) for k in range(2)]

    qkv = jnp.transpose(qkv_weight[0], (1, 0, 2))
    cross = jnp.stack([cross_query_matrix, cross_keyval[:, 0], cross_keyval[:, 1]])
    gen_own = jnp.where(is_image, qkv, cross)
    gen_out_own = jnp.where(is_image, out_weight[0], cross_out)
    if fused:
        x, cot, image_here, qkv_oth, out_oth, gen_oth, gen_out_oth, up_oth, down_oth = route_in(
            count, send_idx, work_idx, home_tokens, home_cot, qkv, out_weight[0], gen_own, gen_out_own, up_weight[0], down_weight[0]
        )
        x, cot, image_here = (value.reshape(rows, width) for value in (x, cot, image_here))
    else:
        got_tokens = travel(home_tokens)
        image_rows = lax.dynamic_slice_in_dim(tokens[0], c * rows, rows)
        image_here = lax.ppermute(image_rows, ("half", "dp", "mp"), pairs)
        got_cot = travel(home_cot)
        gen_oth = swap_mp(gen_own)
        gen_out_oth = swap_mp(gen_out_own)
        qkv_oth = swap_mp(qkv, True)
        out_oth = swap_mp(out_weight[0], True)
        up_oth = swap_mp(up_weight[0])
        down_oth = swap_mp(down_weight[0])
        x = settle(home_tokens, got_tokens)
        cot = settle(home_cot, got_cot)
    gains = norm_gains[0]
    gain_cross = cross_gain[None]
    heads_shape = ((6, rows, 128), BF16)
    wide, narrow = ((rows, width), F32), ((rows, width), BF16)
    head_scratch = pltpu.VMEM((6, rows, 128), BF16)
    bias_scratch = pltpu.VMEM((3, GROUP, GROUP), F32)
    a, r, normed, sq, sk, sv, st = call(
        pre_kernel,
        "pre",
        [narrow, wide, narrow, heads_shape, heads_shape, heads_shape, heads_shape],
        [bias_scratch],
        True,
        meta, x, gains, gain_cross, qkv, qkv_oth, out_weight[0], out_oth,
    )
    b = jnp.where(is_image, a, image_here)
    q, k, v, ctx, sums, mixed, ffn_in = call(
        mid_kernel,
        "mid",
        [heads_shape, heads_shape, heads_shape, heads_shape, ((12, 1, rows), F32), wide, narrow],
        [],
        True,
        meta, a, b, r, gains, gen_own, gen_oth, gen_out_own, gen_out_oth,
    )
    ffn_g_oth, acc_out, acc_grad = ffn_call(False, ffn_in, cot, up_oth, down_oth)
    ffn_g_own, y, gm, gain_ffn = ffn_call(True, ffn_in, cot, up_weight[0], down_weight[0], acc_out, acc_grad, mixed, gains)

    g_own, g_oth, da, db = call(
        back_kernel,
        "back",
        [((4, width, width // 2), BF16), ((4, width, width // 2), BF16), wide, wide],
        [head_scratch] * 4,
        True,
        meta, gm, ctx, sums, q, k, v, a, b, gen_own, gen_oth, gen_out_own, gen_out_oth,
    )
    image_part = lax.ppermute(db.astype(BF16), ("half", "dp", "mp"), [(d, s) for s, d in pairs])

    gt, g3_own, g3_oth, gain_two = call(
        post_kernel,
        "post",
        [wide, ((4, width, width // 2), BF16), ((4, width, width // 2), BF16), ((2, width), F32)],
        [bias_scratch] + [head_scratch] * 4 + [pltpu.VMEM((rows, width), F32)],
        True,
        meta, x, gains, gain_cross, gm, da, db, r, normed, sq, sk, sv, st, qkv, qkv_oth, out_weight[0], out_oth,
    )
    grad_rows = jnp.where(is_image, gt + image_part.astype(F32), gt).astype(BF16)

    if fused:
        gain_mine = jnp.concatenate([gain_two[0:1], gain_ffn, gain_two[1:2], jnp.zeros((5, width), F32)])
        ffn_sum, tower_sum, cross_sum, layer_out, grad_tokens, gain_rows = comm(
            count, back_idx, home_idx, ffn_g_own, ffn_g_oth, g_own, g_oth, g3_own, g3_oth,
            y.reshape(per_core, SLOT, width), grad_rows.reshape(per_core, SLOT, width), gain_mine,
        )
        layer_out, grad_tokens = layer_out.reshape(row_count, width), grad_tokens.reshape(row_count, width)
        gain_rows = lax.dynamic_slice_in_dim(gain_rows, me * (width // count), width // count, axis=1)
        sum_gains, sum_cross_gain = gain_rows[0:2], gain_rows[2]
    else:
        ffn_sum = reduce_dp(ffn_g_own, swap_mp(ffn_g_oth))
        gen_sum = reduce_dp(g_own, swap_mp(g_oth))
        cap_sum = reduce_dp(g3_own, swap_mp(g3_oth))

        def go_home(values):
            own = values.reshape(per_core, SLOT, width)
            other = swap_mp(own)
            packs = gather_slots(back_idx, [own, other], [QCAP // 2] * (SPREAD - 1))
            got = [caption_shift(pack, o + 1) for o, pack in enumerate(packs)]
            more = [swap_mp(g, True) for g in got]
            return gather_slots(home_idx, [own, other] + got + more, [cap_dev])[0].reshape(row_count, width)

        layer_out = go_home(y)
        grad_tokens = go_home(grad_rows).astype(F32)

        zero = jnp.zeros_like(gain_ffn)
        mine = jnp.concatenate([gain_two[0:1], gain_ffn])
        none = jnp.zeros_like(mine)
        gain_rows = jnp.concatenate(
            [jnp.where(is_image, mine, none), jnp.where(is_image, none, mine), gain_two[1:2]]
        )
        gain_rows = lax.psum(gain_rows, ("half", "dp", "mp"))
        part = width // count
        gain_rows = lax.dynamic_slice_in_dim(gain_rows, me * part, part, axis=1)
        sum_gains = jnp.where(is_image, gain_rows[0:2], gain_rows[2:4])
        sum_cross_gain = gain_rows[4]

        cross_low = gen_sum.astype(BF16)
        cross_arrived = lax.ppermute(cross_low, ("half", "dp", "mp"), [(d, s) for s, d in pairs])
        cross_sum = jnp.where(is_image, cross_arrived, cross_low).astype(F32)
        tower_sum = jnp.where(is_image, gen_sum, cap_sum)
    return (
        layer_out[None],
        grad_tokens[None],
        jnp.transpose(tower_sum[1:4], (1, 0, 2))[None],
        tower_sum[0].T[None],
        ffn_sum[0][None],
        ffn_sum[1].T[None],
        sum_gains[None],
        sum_cross_gain,
        cross_sum[1],
        jnp.stack([cross_sum[2], cross_sum[3]], axis=1),
        cross_sum[0].T,
    )


def solution(mesh):
    placed = (
        P("half", "dp", None),
        P("half", None, None, "mp"),
        P("half", "mp", None),
        P("half", None, "mp"),
        P("half", "mp", None),
        P("half", None, None),
        P(),
        P(None, "mp"),
        P(None, None, "mp"),
        P("mp", None),
        P(),
        P(),
        P("half", "dp", None),
    )
    return jax.shard_map(
        shards,
        mesh=mesh,
        in_specs=placed,
        out_specs=(
            P("half", "dp", None),
            P("half", "dp", None),
            P("half", "dp", None, "mp"),
            P("half", "mp", "dp"),
            P("half", "dp", "mp"),
            P("half", "mp", "dp"),
            P("half", None, "dp"),
            P("dp"),
            P("dp", "mp"),
            P("dp", None, "mp"),
            P("mp", "dp"),
        ),
        check_vma=False,
    )
```
